256 devices in a mesh: row: 64 (over y, z, core), col: 4 (over x).
Axes of the slice: x: 4, y: 4, z: 8, core: 2. Of those that a mesh axis runs over, the one named last changes fastest.
Arguments:
- a_tiles: bfloat16 [1024, 27, 128, 128], P('row'), may hold values from -0.109375 to 0.109375
- a_cols: int32 [1024, 27], P('row'), may hold values from 0 to 19, as said below
- p_tiles: bfloat16 [1024, 4, 128, 128], P('row', 'col'), may hold values from -2 to 2
- p_cols: int32 [1024, 4], P('row', 'col'), may hold values from 0 to 127, as said below
- send_rows: int32 [128, 2], P('row'), may hold values from 0 to 15, as said below
Outputs:
- coarse_matrix: float32 [128, 128, 128, 128], P('row', 'col')
The draws below stay inside these ranges and needn't reach their ends.
Inputs may be any that keep to these rules, and one draw needn't show every extreme that they name: `a_cols`: an entry below 16 names a fine block row of the device's own slab; an entry 16 + t with t < 2 names the t-th row that the previous slab sends to this slab, and 18 + t the t-th row that the next slab sends to it. Every slab reads all 4 rows that it receives. Slabs are periodic. `p_cols`: the coarse block column of slot k in fine block row i is congruent to k modulo 4 and lies among the 6 consecutive ids that start at ((i div 16) - 1) * 2, modulo 128. `send_rows`: each row lists 2 distinct slab-local rows.
All inputs are finite; a program needn't handle non-finite values.
Results may differ from the reference program's by a relative error of at most 0.0029.
Values may be sent and summed in bfloat16 or wider, within the bound.
No kernel may reach another device: no remote copies, remote signals or barrier semaphores. Data moves between devices by JAX's collectives and lax.ppermute only.
A program may use at most 192 MiB of HBM per device.

```python
import jax
import jax.numpy as jnp
from jax import lax

TILE = 128
KA = 27
BR = 16
CB = 2
CAPF = 2
KP = 4
NB = 1024
NC = 128
NCC = 32
N_ROW = 64
N_COL = 4


def draw_a_cols(key, part):
    key = jax.random.fold_in(key, 11)
    keys = jax.random.split(key, 3)
    own_refs = jax.random.randint(keys[0], (N_ROW, BR, KA), 0, BR)
    ghost_refs = BR + jax.random.randint(keys[1], (N_ROW, BR, KA), 0, 2 * CAPF)
    selector = jax.random.randint(keys[2], (N_ROW, BR, KA), 0, 3)
    references = jnp.where(selector == 0, ghost_refs, own_refs)
    forced = BR + jnp.arange(2 * CAPF)
    references = references.at[:, BR - 1, 1:1 + 2 * CAPF].set(forced[None, :])
    references = references.at[:, 0, 0].set(0)
    return references.reshape(N_ROW * BR, KA).astype(jnp.int32)


def draw_p_cols(key, part):
    key = jax.random.fold_in(key, 13)
    fine_rows = jnp.arange(NB)
    slab_ids = fine_rows // BR
    slot_ids = jnp.arange(KP)
    window_base = (slab_ids - 1) * CB
    offsets = jnp.mod(slot_ids[None, :] - window_base[:, None], N_COL)
    option_count = (3 * CB - 1 - offsets) // N_COL + 1
    picks = jax.random.randint(key, (NB, KP), 0, 1 << 20) % option_count
    picks = jnp.where((fine_rows % BR == 0)[:, None], 0, picks)
    coarse_ids = jnp.mod(window_base[:, None] + offsets + N_COL * picks, NC)
    return coarse_ids.astype(jnp.int32)


def draw_send_rows(key, part):
    key = jax.random.fold_in(key, 12)
    scores = jax.random.randint(key, (2 * N_ROW, BR), 0, 1 << 20)
    chosen = jnp.argsort(scores, axis=1, stable=True)[:, :CAPF]
    first_list = jnp.concatenate([jnp.array([BR - 1]), jnp.arange(CAPF - 1)])
    chosen = chosen.at[0].set(first_list)
    return chosen.astype(jnp.int32)


def steps_of(key, dims, cuts, least, high):
    def one(axis_at, shards_of):
        draws = jax.random.uniform(jax.random.fold_in(jax.random.fold_in(key, 6), axis_at), (shards_of,), jnp.float32, least / len(cuts), high / len(cuts))
        return jnp.repeat(jnp.exp(draws), dims[axis_at] // shards_of).reshape((-1,) + (1,) * (len(dims) - axis_at - 1))

    loudness = one(*cuts[0])
    for cut in cuts[1:]:
        loudness = loudness * one(*cut)
    return loudness


def centred(stream_key, dims, width, reach, pieces=(), kind=jnp.bfloat16):
    factor_of = steps_of(stream_key, dims, pieces, -0.22, 0.18) if pieces else 1.0
    values = jax.random.normal(stream_key, dims, jnp.float32) * width * factor_of
    return jnp.minimum(jnp.maximum(values, -reach), reach).astype(kind)


def setup_inputs(seed: int = 0) -> dict:
    key_list = jax.random.split(jax.random.key(seed), 6)
    a_tiles = centred(key_list[0], (NB, KA, TILE, TILE), (KA * TILE) ** -0.5, 0.109375, ((0, 64),))
    a_cols = draw_a_cols(jax.random.fold_in(key_list[5], 71), 0)
    p_tiles = centred(key_list[2], (NB, KP, TILE, TILE), (max(TILE // 16, 1)) ** -0.5, 2.0, ((0, 64), (1, 4)))
    p_cols = draw_p_cols(jax.random.fold_in(key_list[5], 71), 0)
    send_rows = draw_send_rows(jax.random.fold_in(key_list[5], 71), 0)
    return {"a_tiles": a_tiles, "a_cols": a_cols, "p_tiles": p_tiles, "p_cols": p_cols, "send_rows": send_rows}


def reference(a_tiles, a_cols, p_tiles, p_cols, send_rows):
    def slab_step(coarse_sum, slab_index):
        first_row = slab_index * BR
        a_block = lax.dynamic_slice_in_dim(a_tiles, first_row, BR, 0).astype(jnp.float32)
        entries = lax.dynamic_slice_in_dim(a_cols, first_row, BR, 0)
        ghost_slot = jnp.clip(entries - BR, 0, 2 * CAPF - 1)
        side = ghost_slot // CAPF
        slot_number = ghost_slot % CAPF
        neighbour = jnp.mod(slab_index + 2 * side - 1, N_ROW).astype(jnp.int32)
        remote = neighbour * BR + send_rows[2 * neighbour + side, slot_number]
        fine_column = jnp.where(entries < BR, first_row + entries, remote).astype(jnp.int32)
        right_tiles = p_tiles[fine_column].astype(jnp.float32)
        right_ids = p_cols[fine_column]
        products = jnp.einsum('imxy,imlyz->imlxz', a_block, right_tiles,
                              precision=lax.Precision.HIGHEST).astype(jnp.bfloat16)
        left_tiles = lax.dynamic_slice_in_dim(p_tiles, first_row, BR, 0).astype(jnp.float32)
        left_ids = lax.dynamic_slice_in_dim(p_cols, first_row, BR, 0)
        tile_terms = jnp.einsum('ikyx,imlyz->ikmlxz', left_tiles, products.astype(jnp.float32),
                                precision=lax.Precision.HIGHEST)
        row_ids = jnp.broadcast_to(left_ids[:, :, None, None], tile_terms.shape[:4])
        column_ids = (right_ids % N_COL) * NCC + right_ids // N_COL
        column_ids = jnp.broadcast_to(column_ids[:, None, :, :], tile_terms.shape[:4])
        return coarse_sum.at[row_ids, column_ids].add(tile_terms), None

    zero_matrix = jnp.zeros((NC, NC, TILE, TILE), jnp.float32)
    result, unused = lax.scan(slab_step, zero_matrix, jnp.arange(N_ROW, dtype=jnp.int32))
    return result
```

```python
import functools

import jax
import jax.numpy as jnp
from jax import lax
from jax.experimental import pallas as pl
from jax.experimental.pallas import tpu as pltpu
from jax.sharding import PartitionSpec as P

T = 128
BR = 16
KA = 27
G = 3
UNROLL = 2
NCC = 32
F32 = jnp.float32
BF16 = jnp.bfloat16
MB = 1 << 20
SMEM = pl.BlockSpec(memory_space=pltpu.SMEM)
VMEM = pl.BlockSpec(memory_space=pltpu.VMEM)
HBM = pl.BlockSpec(memory_space=pl.ANY)
FIXED = pl.BlockSpec(memory_space=pltpu.HBM)


def place():
    s = lax.axis_index("row")
    c = lax.axis_index("col")
    d = lax.rem(c - 2 * s + 512, 4)
    is_n = d >= 2
    number = lax.rem(d, 2)
    return s, is_n, number, 2 * s - 4 + d


def roles(s):
    return (2, 3, 1, 0) if s % 2 == 0 else (0, 1, 3, 2)


def send(block, routes, rows, cols):
    pairs = []
    for s in range(rows):
        at = roles(s)
        pairs += [(s * cols + at[i], s * cols + at[j]) for i, j in routes]
    return lax.ppermute(block, ("row", "col"), pairs)


def swap_rows(block, odd, rows, cols):
    pairs = [(s, (s + 1) % rows if s % 2 == odd else (s - 1) % rows) for s in range(rows)]
    return lax.ppermute(block, "row", pairs)


N1, N2, L1, L2 = range(4)


def note_kernel(ids_ref, p_ref, all_ref, sem):
    copy = pltpu.make_async_copy(p_ref, all_ref.at[pl.ds(0, BR)], sem)
    copy.start()
    for i in range(BR):
        all_ref[BR, 8 * i:8 * i + 8, :] = jnp.full((8, T), ids_ref[i].astype(F32), F32).astype(BF16)
    copy.wait()


def pick_kernel(send_ref, p_ref, near_ref, far_ref, sems):
    odd = lax.rem(lax.axis_index("row"), 2)
    copies = []
    for d, out in ((odd, near_ref), (1 - odd, far_ref)):
        for t in range(2):
            row = send_ref[d, t]
            copies.append(pltpu.make_async_copy(p_ref.at[row], out.at[t], sems.at[len(copies)]))
            copies.append(pltpu.make_async_copy(p_ref.at[BR, pl.ds(pl.multiple_of(row * 8, 8), 8)],
                                                out.at[2, pl.ds(t * 8, 8)], sems.at[len(copies)]))
    for copy in copies:
        copy.start()
    for copy in copies:
        copy.wait()


def product_kernel(cols_ref, ids_ref, a_ref, own_ref, near_ref, far_ref, sums_ref, tiles, right, own, ghosts, sems):
    early = [pltpu.make_async_copy(own_ref.at[pl.ds(0, BR)], own, sems.at[BR]),
             pltpu.make_async_copy(near_ref, ghosts.at[0], sems.at[BR + 1]),
             pltpu.make_async_copy(far_ref, ghosts.at[1], sems.at[BR + 2])]
    for copy in early:
        copy.start()
    for i in range(BR):
        pltpu.make_async_copy(a_ref.at[i], tiles.at[i], sems.at[i]).start()
    s, is_n, number, first = place()
    right[...] = jnp.zeros_like(right)
    for copy in early:
        copy.wait()
    for j in range(BR):
        group = lax.rem(ids_ref[j] - first + 512, T) // 4
        right[j * G + group] = own[j]
    odd = lax.rem(s, 2)
    for side in range(2):
        base = BR + 2 * (1 - odd if side == 0 else odd)
        for t in range(2):
            ids = ghosts[side, 2, 8 * t:8 * t + 8, :].astype(F32)[:1]
            tile = ghosts[side, t].astype(F32)
            for g in range(G):
                wanted = lax.rem(first + 4 * g + T, T).astype(F32)
                right[(base + t) * G + g] = jnp.where(ids == wanted, tile, 0.0).astype(BF16)

    def one(i):
        pltpu.make_async_copy(a_ref.at[i], tiles.at[i], sems.at[i]).wait()
        rows = [cols_ref[i, m] * G for m in range(KA)]
        left = jnp.concatenate([tiles[i, m] for m in range(KA)], axis=1)
        both = jnp.concatenate(
            [jnp.concatenate([right[j + g] for g in range(G)], axis=1) for j in rows], axis=0)
        acc = jnp.dot(left, both, preferred_element_type=F32)
        turned = jnp.concatenate([acc[:, g * T:(g + 1) * T].T for g in range(G)], axis=0)
        sums_ref[i] = turned.astype(BF16)

    def step(n, _):
        for k in range(UNROLL):
            one(UNROLL * n + k)
        return 0

    lax.fori_loop(0, BR // UNROLL, step, 0)


def wide(ref):
    return jnp.concatenate([ref[i] for i in range(BR)], axis=1)


def partial_kernel(sums_ref, own, swapped, across, crossed, near_ref, far_ref, tiles, masked, sems):
    s, is_n, number, first = place()

    @pl.when(is_n)
    def _():
        for n, src in enumerate((own, swapped)):
            pltpu.make_async_copy(src, tiles.at[n], sems.at[n]).start()

    @pl.when(jnp.logical_not(is_n))
    def _():
        for n, src in enumerate((across, crossed)):
            pltpu.make_async_copy(src, tiles.at[n], sems.at[n]).start()

    sums = wide(sums_ref)
    odd = lax.rem(s, 2) == 1
    first_row = jnp.where(is_n, number, 1 - number)
    for n in range(2):
        pltpu.make_async_copy(own, tiles.at[n], sems.at[n]).wait()
        row = first_row if n == 0 else 1 - first_row
        wanted = lax.rem(2 * s - 2 + row + T, T).astype(F32)
        for i in range(BR):
            lower = tiles[n, BR, 8 * i:8 * i + 8, :].astype(F32)[:1] == wanted
            tile = tiles[n, i].astype(F32)
            masked[n, i * T:(i + 1) * T, :T] = jnp.where(lower, tile, 0.0).astype(BF16)
            masked[n, i * T:(i + 1) * T, T:] = jnp.where(lower, 0.0, tile).astype(BF16)
        terms = jnp.dot(sums, masked[n], preferred_element_type=F32)
        near_ref[row] = jnp.where(odd, terms[:, :T], terms[:, T:])
        far_ref[row] = jnp.where(odd, terms[:, T:], terms[:, :T])


def local_kernel(sums_ref, own, swapped, across, crossed, after, out_ref, total_ref, tiles, zeros, sems):
    del after
    s, is_n, number, first = place()

    @pl.when(is_n)
    def _():
        for n, src in enumerate((across, crossed)):
            pltpu.make_async_copy(src, tiles.at[n], sems.at[n]).start()

    @pl.when(jnp.logical_not(is_n))
    def _():
        for n, src in enumerate((own, swapped)):
            pltpu.make_async_copy(src, tiles.at[n], sems.at[n]).start()

    zeros[...] = jnp.zeros_like(zeros)
    copies = [pltpu.make_async_copy(zeros, out_ref.at[r, pl.ds(q, 8)], sems.at[2 + r * 4 + q // 8])
              for r in range(2) for q in range(0, NCC, 8)]
    for copy in copies:
        copy.start()
    total_ref[...] = jnp.zeros_like(total_ref)
    sums = wide(sums_ref)
    at = pl.ds(pl.multiple_of(is_n.astype(jnp.int32) * T, T), G * T)
    first_row = jnp.where(is_n, 1 - number, number)
    for n in range(2):
        pltpu.make_async_copy(own, tiles.at[n], sems.at[n]).wait()
        right = tiles[n, :BR].reshape(BR * T, T)
        row = first_row if n == 0 else 1 - first_row
        total_ref[row, at, :] = jnp.dot(sums, right, preferred_element_type=F32)
    for copy in copies:
        copy.wait()


def final_kernel(total_ref, near_ref, far_ref, zeroed, out_ref, blocks, sems):
    del zeroed
    s, is_n, number, first = place()
    base = jnp.where(is_n, first - 4, first)
    odd = lax.rem(s, 2) == 1
    copies = []
    for r in range(2):
        for q in range(4):
            block = total_ref[r, q * T:(q + 1) * T, :]
            if q < G:
                at = slice(q * T, (q + 1) * T)
                block += jnp.where(odd, near_ref[r, at, :], far_ref[r, at, :])
            if q > 0:
                at = slice((q - 1) * T, q * T)
                block += jnp.where(odd, far_ref[r, at, :], near_ref[r, at, :])
            blocks[r, q] = block.T
            column = lax.rem(base + 4 * q + T, T) // 4
            copy = pltpu.make_async_copy(blocks.at[r, q], out_ref.at[r, column], sems.at[r * 4 + q])
            copy.start()
            copies.append(copy)
    for copy in copies:
        copy.wait()


def params(mib):
    return pltpu.CompilerParams(vmem_limit_bytes=mib * MB)


def cost(flops, count):
    return pl.CostEstimate(flops=flops, bytes_accessed=count, transcendentals=0)


def shards(rows, cols, a_tiles, a_cols, p_tiles, p_cols, send_rows):
    go = functools.partial(send, rows=rows, cols=cols)
    own = p_tiles.reshape(BR, T, T)
    ids = p_cols.reshape(BR)
    noted = pl.pallas_call(
        note_kernel, out_shape=jax.ShapeDtypeStruct((BR + 1, T, T), BF16), in_specs=[SMEM, FIXED], out_specs=VMEM,
        scratch_shapes=[pltpu.SemaphoreType.DMA], compiler_params=params(8), name="note",
    )(ids, own)
    swapped = go(noted, ((N1, N2), (N2, N1), (L1, L2), (L2, L1)))
    across = go(noted, ((N1, L1), (N2, L2), (L1, N1), (L2, N2)))
    crossed = go(noted, ((N1, L2), (N2, L1), (L1, N2), (L2, N1)))
    swapped_late, across_late, crossed_late = swapped, across, crossed
    ghost = jax.ShapeDtypeStruct((3, T, T), BF16)
    near, far = pl.pallas_call(
        pick_kernel, out_shape=(ghost, ghost), in_specs=[SMEM, HBM], out_specs=(VMEM, VMEM),
        scratch_shapes=[pltpu.SemaphoreType.DMA((8,))], compiler_params=params(8), name="pick",
    )(send_rows, noted)
    near, far = swap_rows(near, 0, rows, cols), swap_rows(far, 1, rows, cols)
    sums = pl.pallas_call(
        product_kernel, out_shape=jax.ShapeDtypeStruct((BR, G * T, T), BF16),
        in_specs=[SMEM, SMEM, FIXED, HBM, HBM, HBM], out_specs=VMEM,
        scratch_shapes=[pltpu.VMEM((BR, KA, T, T), BF16), pltpu.VMEM(((BR + 4) * G, T, T), BF16),
                        pltpu.VMEM((BR, T, T), BF16), pltpu.VMEM((2, 3, T, T), BF16),
                        pltpu.SemaphoreType.DMA((BR + 3,))],
        compiler_params=params(50), cost_estimate=cost(7_000_000_000, 15_000_000), name="products",
    )(a_cols, ids, a_tiles, noted, near, far)
    travels = jax.ShapeDtypeStruct((2, G * T, T), F32)
    near, far = pl.pallas_call(
        partial_kernel, out_shape=(travels, travels), in_specs=[VMEM] + [HBM] * 4, out_specs=(VMEM, VMEM),
        scratch_shapes=[pltpu.VMEM((2, BR + 1, T, T), BF16), pltpu.VMEM((2, BR * T, 2 * T), BF16),
                        pltpu.SemaphoreType.DMA((2,))],
        compiler_params=params(24), name="partials",
    )(sums, noted, swapped, across, crossed)
    near_sum, far_sum = swap_rows(near, 0, rows, cols), swap_rows(far, 1, rows, cols)
    out = jax.ShapeDtypeStruct((2, NCC, T, T), F32)
    zeroed, total = pl.pallas_call(
        local_kernel, out_shape=(out, jax.ShapeDtypeStruct((2, 4 * T, T), F32)),
        in_specs=[VMEM] + [HBM] * 5, out_specs=(HBM, VMEM),
        scratch_shapes=[pltpu.VMEM((2, BR + 1, T, T), BF16), pltpu.VMEM((8, T, T), F32),
                        pltpu.SemaphoreType.DMA((10,))],
        compiler_params=params(24), name="local",
    )(sums, noted, swapped_late, across_late, crossed_late, near)
    return pl.pallas_call(
        final_kernel, out_shape=out, in_specs=[VMEM] * 3 + [HBM], out_specs=HBM,
        scratch_shapes=[pltpu.VMEM((2, 4, T, T), F32), pltpu.SemaphoreType.DMA((8,))],
        input_output_aliases={3: 0}, compiler_params=params(24), name="final",
    )(total, near_sum, far_sum, zeroed)


def solution(mesh):
    in_specs = (P("row", None, None, None), P("row", None), P("row", "col", None, None), P("row", "col"), P("row", None))
    body = functools.partial(shards, mesh.shape["row"], mesh.shape["col"])
    return jax.shard_map(body, mesh=mesh, in_specs=in_specs, out_specs=P("row", "col", None, None), check_vma=False)
```

```python
import functools

import jax
import jax.numpy as jnp
from jax import lax
from jax.experimental import pallas as pl
from jax.experimental.pallas import tpu as pltpu
from jax.sharding import PartitionSpec as P

T = 128
BR = 16
KA = 27
G = 3
UNROLL = 2
NCC = 32
F32 = jnp.float32
BF16 = jnp.bfloat16
MB = 1 << 20
SMEM = pl.BlockSpec(memory_space=pltpu.SMEM)
VMEM = pl.BlockSpec(memory_space=pltpu.VMEM)
HBM = pl.BlockSpec(memory_space=pl.ANY)
FIXED = pl.BlockSpec(memory_space=pltpu.HBM)


def place():
    s = lax.axis_index("row")
    c = lax.axis_index("col")
    d = lax.rem(c - 2 * s + 512, 4)
    is_n = d >= 2
    number = lax.rem(d, 2)
    return s, is_n, number, 2 * s - 4 + d


def roles(s):
    return (2, 3, 1, 0) if s % 2 == 0 else (0, 1, 3, 2)


def send(block, routes, rows, cols):
    pairs = []
    for s in range(rows):
        at = roles(s)
        pairs += [(s * cols + at[i], s * cols + at[j]) for i, j in routes]
    return lax.ppermute(block, ("row", "col"), pairs)


def swap_rows(block, odd, rows, cols):
    pairs = [(s, (s + 1) % rows if s % 2 == odd else (s - 1) % rows) for s in range(rows)]
    return lax.ppermute(block, "row", pairs)


N1, N2, L1, L2 = range(4)


def note_kernel(ids_ref, p_ref, all_ref, sem):
    copy = pltpu.make_async_copy(p_ref, all_ref.at[pl.ds(0, BR)], sem)
    copy.start()
    for i in range(BR):
        all_ref[BR, 8 * i:8 * i + 8, :] = jnp.full((8, T), ids_ref[i].astype(F32), F32).astype(BF16)
    copy.wait()


def pick_kernel(send_ref, p_ref, near_ref, far_ref, sems):
    odd = lax.rem(lax.axis_index("row"), 2)
    copies = []
    for d, out in ((odd, near_ref), (1 - odd, far_ref)):
        for t in range(2):
            row = send_ref[d, t]
            copies.append(pltpu.make_async_copy(p_ref.at[row], out.at[t], sems.at[len(copies)]))
            copies.append(pltpu.make_async_copy(p_ref.at[BR, pl.ds(pl.multiple_of(row * 8, 8), 8)],
                                                out.at[2, pl.ds(t * 8, 8)], sems.at[len(copies)]))
    for copy in copies:
        copy.start()
    for copy in copies:
        copy.wait()


def product_kernel(cols_ref, ids_ref, a_ref, own_ref, near_ref, far_ref, sums_ref, rest_ref, tiles, right, own, ghosts, sems):
    early = [pltpu.make_async_copy(own_ref.at[pl.ds(0, BR)], own, sems.at[BR]),
             pltpu.make_async_copy(near_ref, ghosts.at[0], sems.at[BR + 1]),
             pltpu.make_async_copy(far_ref, ghosts.at[1], sems.at[BR + 2])]
    for copy in early:
        copy.start()
    for i in range(BR):
        pltpu.make_async_copy(a_ref.at[i], tiles.at[i], sems.at[i]).start()
    s, is_n, number, first = place()
    right[...] = jnp.zeros_like(right)
    for copy in early:
        copy.wait()
    for j in range(BR):
        group = lax.rem(ids_ref[j] - first + 512, T) // 4
        right[j * G + group] = own[j]
    odd = lax.rem(s, 2)
    for side in range(2):
        base = BR + 2 * (1 - odd if side == 0 else odd)
        for t in range(2):
            ids = ghosts[side, 2, 8 * t:8 * t + 8, :].astype(F32)[:1]
            tile = ghosts[side, t].astype(F32)
            for g in range(G):
                wanted = lax.rem(first + 4 * g + T, T).astype(F32)
                right[(base + t) * G + g] = jnp.where(ids == wanted, tile, 0.0).astype(BF16)

    def one(i):
        pltpu.make_async_copy(a_ref.at[i], tiles.at[i], sems.at[i]).wait()
        rows = [cols_ref[i, m] * G for m in range(KA)]
        left = jnp.concatenate([tiles[i, m] for m in range(KA)], axis=1)
        both = jnp.concatenate(
            [jnp.concatenate([right[j + g] for g in range(G)], axis=1) for j in rows], axis=0)
        acc = jnp.dot(left, both, preferred_element_type=F32)
        turned = jnp.concatenate([acc[:, g * T:(g + 1) * T].T for g in range(G)], axis=0)
        high = turned.astype(BF16)
        sums_ref[i] = high
        rest_ref[i] = (turned - high.astype(F32)).astype(BF16)

    def step(n, _):
        for k in range(UNROLL):
            one(UNROLL * n + k)
        return 0

    lax.fori_loop(0, BR // UNROLL, step, 0)


def wide(ref):
    return jnp.concatenate([ref[i] for i in range(BR)], axis=1)


def partial_kernel(sums_ref, own, swapped, across, crossed, near_ref, far_ref, tiles, masked, sems):
    s, is_n, number, first = place()

    @pl.when(is_n)
    def _():
        for n, src in enumerate((own, swapped)):
            pltpu.make_async_copy(src, tiles.at[n], sems.at[n]).start()

    @pl.when(jnp.logical_not(is_n))
    def _():
        for n, src in enumerate((across, crossed)):
            pltpu.make_async_copy(src, tiles.at[n], sems.at[n]).start()

    sums = wide(sums_ref)
    odd = lax.rem(s, 2) == 1
    first_row = jnp.where(is_n, number, 1 - number)
    for n in range(2):
        pltpu.make_async_copy(own, tiles.at[n], sems.at[n]).wait()
        row = first_row if n == 0 else 1 - first_row
        wanted = lax.rem(2 * s - 2 + row + T, T).astype(F32)
        for i in range(BR):
            lower = tiles[n, BR, 8 * i:8 * i + 8, :].astype(F32)[:1] == wanted
            tile = tiles[n, i].astype(F32)
            masked[n, i * T:(i + 1) * T, :T] = jnp.where(lower, tile, 0.0).astype(BF16)
            masked[n, i * T:(i + 1) * T, T:] = jnp.where(lower, 0.0, tile).astype(BF16)
        terms = jnp.dot(sums, masked[n], preferred_element_type=F32)
        near_ref[row] = jnp.where(odd, terms[:, :T], terms[:, T:]).astype(BF16)
        far_ref[row] = jnp.where(odd, terms[:, T:], terms[:, :T]).astype(BF16)


def local_kernel(sums_ref, rest_ref, own, swapped, across, crossed, after, out_ref, total_ref, tiles, zeros, sems):
    del after
    s, is_n, number, first = place()

    @pl.when(is_n)
    def _():
        for n, src in enumerate((across, crossed)):
            pltpu.make_async_copy(src, tiles.at[n], sems.at[n]).start()

    @pl.when(jnp.logical_not(is_n))
    def _():
        for n, src in enumerate((own, swapped)):
            pltpu.make_async_copy(src, tiles.at[n], sems.at[n]).start()

    zeros[...] = jnp.zeros_like(zeros)
    copies = [pltpu.make_async_copy(zeros, out_ref.at[r, pl.ds(q, 8)], sems.at[2 + r * 4 + q // 8])
              for r in range(2) for q in range(0, NCC, 8)]
    for copy in copies:
        copy.start()
    total_ref[...] = jnp.zeros_like(total_ref)
    sums = wide(sums_ref)
    at = pl.ds(pl.multiple_of(is_n.astype(jnp.int32) * T, T), G * T)
    first_row = jnp.where(is_n, 1 - number, number)
    for n in range(2):
        pltpu.make_async_copy(own, tiles.at[n], sems.at[n]).wait()
        right = tiles[n, :BR].reshape(BR * T, T)
        row = first_row if n == 0 else 1 - first_row
        total_ref[row, at, :] = (jnp.dot(sums, right, preferred_element_type=F32)
                                 + jnp.dot(wide(rest_ref), right, preferred_element_type=F32))
    for copy in copies:
        copy.wait()


def final_kernel(total_ref, near_ref, far_ref, zeroed, out_ref, blocks, sems):
    del zeroed
    s, is_n, number, first = place()
    base = jnp.where(is_n, first - 4, first)
    odd = lax.rem(s, 2) == 1
    copies = []
    for r in range(2):
        for q in range(4):
            block = total_ref[r, q * T:(q + 1) * T, :]
            if q < G:
                at = slice(q * T, (q + 1) * T)
                block += jnp.where(odd, near_ref[r, at, :].astype(F32), far_ref[r, at, :].astype(F32))
            if q > 0:
                at = slice((q - 1) * T, q * T)
                block += jnp.where(odd, far_ref[r, at, :].astype(F32), near_ref[r, at, :].astype(F32))
            blocks[r, q] = block.T
            column = lax.rem(base + 4 * q + T, T) // 4
            copy = pltpu.make_async_copy(blocks.at[r, q], out_ref.at[r, column], sems.at[r * 4 + q])
            copy.start()
            copies.append(copy)
    for copy in copies:
        copy.wait()


def params(mib):
    return pltpu.CompilerParams(vmem_limit_bytes=mib * MB)


def cost(flops, count):
    return pl.CostEstimate(flops=flops, bytes_accessed=count, transcendentals=0)


def shards(rows, cols, a_tiles, a_cols, p_tiles, p_cols, send_rows):
    go = functools.partial(send, rows=rows, cols=cols)
    own = p_tiles.reshape(BR, T, T)
    ids = p_cols.reshape(BR)
    noted = pl.pallas_call(
        note_kernel, out_shape=jax.ShapeDtypeStruct((BR + 1, T, T), BF16), in_specs=[SMEM, FIXED], out_specs=VMEM,
        scratch_shapes=[pltpu.SemaphoreType.DMA], compiler_params=params(8), name="note",
    )(ids, own)
    swapped = go(noted, ((N1, N2), (N2, N1), (L1, L2), (L2, L1)))
    across = go(noted, ((N1, L1), (N2, L2), (L1, N1), (L2, N2)))
    crossed = go(noted, ((N1, L2), (N2, L1), (L1, N2), (L2, N1)))
    ghost = jax.ShapeDtypeStruct((3, T, T), BF16)
    near, far = pl.pallas_call(
        pick_kernel, out_shape=(ghost, ghost), in_specs=[SMEM, HBM], out_specs=(VMEM, VMEM),
        scratch_shapes=[pltpu.SemaphoreType.DMA((8,))], compiler_params=params(8), name="pick",
    )(send_rows, noted)
    near, far = swap_rows(near, 0, rows, cols), swap_rows(far, 1, rows, cols)
    turned = jax.ShapeDtypeStruct((BR, G * T, T), BF16)
    sums, rest = pl.pallas_call(
        product_kernel, out_shape=(turned, turned),
        in_specs=[SMEM, SMEM, FIXED, HBM, HBM, HBM], out_specs=(VMEM, VMEM),
        scratch_shapes=[pltpu.VMEM((BR, KA, T, T), BF16), pltpu.VMEM(((BR + 4) * G, T, T), BF16),
                        pltpu.VMEM((BR, T, T), BF16), pltpu.VMEM((2, 3, T, T), BF16),
                        pltpu.SemaphoreType.DMA((BR + 3,))],
        compiler_params=params(50), name="products",
    )(a_cols, ids, a_tiles, noted, near, far)
    travels = jax.ShapeDtypeStruct((2, G * T, T), BF16)
    near, far = pl.pallas_call(
        partial_kernel, out_shape=(travels, travels), in_specs=[VMEM] + [HBM] * 4, out_specs=(VMEM, VMEM),
        scratch_shapes=[pltpu.VMEM((2, BR + 1, T, T), BF16), pltpu.VMEM((2, BR * T, 2 * T), BF16),
                        pltpu.SemaphoreType.DMA((2,))],
        compiler_params=params(24), name="partials",
    )(sums, noted, swapped, across, crossed)
    near_sum, far_sum = swap_rows(near, 0, rows, cols), swap_rows(far, 1, rows, cols)
    out = jax.ShapeDtypeStruct((2, NCC, T, T), F32)
    zeroed, total = pl.pallas_call(
        local_kernel, out_shape=(out, jax.ShapeDtypeStruct((2, 4 * T, T), F32)),
        in_specs=[VMEM] * 2 + [HBM] * 5, out_specs=(HBM, VMEM),
        scratch_shapes=[pltpu.VMEM((2, BR + 1, T, T), BF16), pltpu.VMEM((8, T, T), F32),
                        pltpu.SemaphoreType.DMA((10,))],
        compiler_params=params(24), name="local",
    )(sums, rest, noted, swapped, across, crossed, near)
    return pl.pallas_call(
        final_kernel, out_shape=out, in_specs=[VMEM] * 3 + [HBM], out_specs=HBM,
        scratch_shapes=[pltpu.VMEM((2, 4, T, T), F32), pltpu.SemaphoreType.DMA((8,))],
        input_output_aliases={3: 0}, compiler_params=params(24), name="final",
    )(total, near_sum, far_sum, zeroed)


def solution(mesh):
    in_specs = (P("row", None, None, None), P("row", None), P("row", "col", None, None), P("row", "col"), P("row", None))
    body = functools.partial(shards, mesh.shape["row"], mesh.shape["col"])
    return jax.shard_map(body, mesh=mesh, in_specs=in_specs, out_specs=P("row", "col", None, None), check_vma=False)
```

```python
import functools

import jax
import jax.numpy as jnp
from jax import lax
from jax.experimental import pallas as pl
from jax.experimental.pallas import tpu as pltpu
from jax.sharding import PartitionSpec as P

T = 128
BR = 16
KA = 27
G = 3
UNROLL = 2
NCC = 32
F32 = jnp.float32
BF16 = jnp.bfloat16
MB = 1 << 20
SMEM = pl.BlockSpec(memory_space=pltpu.SMEM)
VMEM = pl.BlockSpec(memory_space=pltpu.VMEM)
HBM = pl.BlockSpec(memory_space=pl.ANY)
FIXED = pl.BlockSpec(memory_space=pltpu.HBM)


def place():
    s = lax.axis_index("row")
    c = lax.axis_index("col")
    d = lax.rem(c - 2 * s + 512, 4)
    is_n = d >= 2
    number = lax.rem(d, 2)
    return s, is_n, number, 2 * s - 4 + d


def roles(s):
    return (2, 3, 1, 0) if s % 2 == 0 else (0, 1, 3, 2)


def send(block, routes, rows, cols):
    pairs = []
    for s in range(rows):
        at = roles(s)
        pairs += [(s * cols + at[i], s * cols + at[j]) for i, j in routes]
    return lax.ppermute(block, ("row", "col"), pairs)


def swap_rows(block, odd, rows, cols):
    pairs = [(s, (s + 1) % rows if s % 2 == odd else (s - 1) % rows) for s in range(rows)]
    return lax.ppermute(block, "row", pairs)


N1, N2, L1, L2 = range(4)


def note_kernel(ids_ref, p_ref, all_ref, sem):
    copy = pltpu.make_async_copy(p_ref, all_ref.at[pl.ds(0, BR)], sem)
    copy.start()
    for i in range(BR):
        all_ref[BR, 8 * i:8 * i + 8, :] = jnp.full((8, T), ids_ref[i].astype(F32), F32).astype(BF16)
    copy.wait()


def pick_kernel(send_ref, p_ref, near_ref, far_ref, sems):
    odd = lax.rem(lax.axis_index("row"), 2)
    copies = []
    for d, out in ((odd, near_ref), (1 - odd, far_ref)):
        for t in range(2):
            row = send_ref[d, t]
            copies.append(pltpu.make_async_copy(p_ref.at[row], out.at[t], sems.at[len(copies)]))
            copies.append(pltpu.make_async_copy(p_ref.at[BR, pl.ds(pl.multiple_of(row * 8, 8), 8)],
                                                out.at[2, pl.ds(t * 8, 8)], sems.at[len(copies)]))
    for copy in copies:
        copy.start()
    for copy in copies:
        copy.wait()


def product_kernel(cols_ref, ids_ref, a_ref, own_ref, near_ref, far_ref, sums_ref, rest_ref, tiles, right, own, ghosts, sems):
    early = [pltpu.make_async_copy(own_ref.at[pl.ds(0, BR)], own, sems.at[BR]),
             pltpu.make_async_copy(near_ref, ghosts.at[0], sems.at[BR + 1]),
             pltpu.make_async_copy(far_ref, ghosts.at[1], sems.at[BR + 2])]
    for copy in early:
        copy.start()
    for i in range(BR):
        pltpu.make_async_copy(a_ref.at[i], tiles.at[i], sems.at[i]).start()
    s, is_n, number, first = place()
    right[...] = jnp.zeros_like(right)
    for copy in early:
        copy.wait()
    for j in range(BR):
        group = lax.rem(ids_ref[j] - first + 512, T) // 4
        right[j * G + group] = own[j]
    odd = lax.rem(s, 2)
    for side in range(2):
        base = BR + 2 * (1 - odd if side == 0 else odd)
        for t in range(2):
            ids = ghosts[side, 2, 8 * t:8 * t + 8, :].astype(F32)[:1]
            tile = ghosts[side, t].astype(F32)
            for g in range(G):
                wanted = lax.rem(first + 4 * g + T, T).astype(F32)
                right[(base + t) * G + g] = jnp.where(ids == wanted, tile, 0.0).astype(BF16)

    def one(i):
        pltpu.make_async_copy(a_ref.at[i], tiles.at[i], sems.at[i]).wait()
        rows = [cols_ref[i, m] * G for m in range(KA)]
        left = jnp.concatenate([tiles[i, m] for m in range(KA)], axis=1)
        both = jnp.concatenate(
            [jnp.concatenate([right[j + g] for g in range(G)], axis=1) for j in rows], axis=0)
        acc = jnp.dot(left, both, preferred_element_type=F32)
        turned = jnp.concatenate([acc[:, g * T:(g + 1) * T].T for g in range(G)], axis=0)
        high = turned.astype(BF16)
        sums_ref[i] = high
        rest_ref[i] = (turned - high.astype(F32)).astype(BF16)

    def step(n, _):
        for k in range(UNROLL):
            one(UNROLL * n + k)
        return 0

    lax.fori_loop(0, BR // UNROLL, step, 0)


def wide(ref):
    return jnp.concatenate([ref[i] for i in range(BR)], axis=1)


def partial_kernel(sums_ref, own, swapped, across, crossed, near_ref, far_ref, tiles, masked, sems):
    s, is_n, number, first = place()

    @pl.when(is_n)
    def _():
        for n, src in enumerate((own, swapped)):
            pltpu.make_async_copy(src, tiles.at[n], sems.at[n]).start()

    @pl.when(jnp.logical_not(is_n))
    def _():
        for n, src in enumerate((across, crossed)):
            pltpu.make_async_copy(src, tiles.at[n], sems.at[n]).start()

    sums = wide(sums_ref)
    odd = lax.rem(s, 2) == 1
    first_row = jnp.where(is_n, number, 1 - number)
    for n in range(2):
        pltpu.make_async_copy(own, tiles.at[n], sems.at[n]).wait()
        row = first_row if n == 0 else 1 - first_row
        wanted = lax.rem(2 * s - 2 + row + T, T).astype(F32)
        for i in range(BR):
            lower = tiles[n, BR, 8 * i:8 * i + 8, :].astype(F32)[:1] == wanted
            tile = tiles[n, i].astype(F32)
            masked[n, i * T:(i + 1) * T, :T] = jnp.where(lower, tile, 0.0).astype(BF16)
            masked[n, i * T:(i + 1) * T, T:] = jnp.where(lower, 0.0, tile).astype(BF16)
        terms = jnp.dot(sums, masked[n], preferred_element_type=F32)
        near_ref[row] = jnp.where(odd, terms[:, :T], terms[:, T:]).astype(BF16)
        far_ref[row] = jnp.where(odd, terms[:, T:], terms[:, :T]).astype(BF16)


def local_kernel(sums_ref, rest_ref, own, swapped, across, crossed, after, out_ref, total_ref, tiles, zeros, sems):
    del after
    s, is_n, number, first = place()

    @pl.when(is_n)
    def _():
        for n, src in enumerate((across, crossed)):
            pltpu.make_async_copy(src, tiles.at[n], sems.at[n]).start()

    @pl.when(jnp.logical_not(is_n))
    def _():
        for n, src in enumerate((own, swapped)):
            pltpu.make_async_copy(src, tiles.at[n], sems.at[n]).start()

    zeros[...] = jnp.zeros_like(zeros)
    copies = [pltpu.make_async_copy(zeros, out_ref.at[r, pl.ds(q, 8)], sems.at[2 + r * 4 + q // 8])
              for r in range(2) for q in range(0, NCC, 8)]
    for copy in copies:
        copy.start()
    total_ref[...] = jnp.zeros_like(total_ref)
    sums = wide(sums_ref)
    at = pl.ds(pl.multiple_of(is_n.astype(jnp.int32) * T, T), G * T)
    first_row = jnp.where(is_n, 1 - number, number)
    for n in range(2):
        pltpu.make_async_copy(own, tiles.at[n], sems.at[n]).wait()
    right = jnp.concatenate([tiles[n, :BR].reshape(BR * T, T) for n in range(2)], axis=1)
    terms = jnp.dot(sums, right, preferred_element_type=F32)
    terms += jnp.dot(wide(rest_ref), right, preferred_element_type=F32)
    total_ref[first_row, at, :] = terms[:, :T]
    total_ref[1 - first_row, at, :] = terms[:, T:]
    for copy in copies:
        copy.wait()


def final_kernel(total_ref, near_ref, far_ref, zeroed, out_ref, blocks, sems):
    del zeroed
    s, is_n, number, first = place()
    base = jnp.where(is_n, first - 4, first)
    odd = lax.rem(s, 2) == 1
    copies = []
    for r in range(2):
        for q in range(4):
            block = total_ref[r, q * T:(q + 1) * T, :]
            if q < G:
                at = slice(q * T, (q + 1) * T)
                block += jnp.where(odd, near_ref[r, at, :].astype(F32), far_ref[r, at, :].astype(F32))
            if q > 0:
                at = slice((q - 1) * T, q * T)
                block += jnp.where(odd, far_ref[r, at, :].astype(F32), near_ref[r, at, :].astype(F32))
            blocks[r, q] = block.T
            column = lax.rem(base + 4 * q + T, T) // 4
            copy = pltpu.make_async_copy(blocks.at[r, q], out_ref.at[r, column], sems.at[r * 4 + q])
            copy.start()
            copies.append(copy)
    for copy in copies:
        copy.wait()


def params(mib):
    return pltpu.CompilerParams(vmem_limit_bytes=mib * MB)


def cost(flops, count):
    return pl.CostEstimate(flops=flops, bytes_accessed=count, transcendentals=0)


def shards(rows, cols, a_tiles, a_cols, p_tiles, p_cols, send_rows):
    go = functools.partial(send, rows=rows, cols=cols)
    own = p_tiles.reshape(BR, T, T)
    ids = p_cols.reshape(BR)
    noted = pl.pallas_call(
        note_kernel, out_shape=jax.ShapeDtypeStruct((BR + 1, T, T), BF16), in_specs=[SMEM, FIXED], out_specs=VMEM,
        scratch_shapes=[pltpu.SemaphoreType.DMA], compiler_params=params(8), name="note",
    )(ids, own)
    swapped = go(noted, ((N1, N2), (N2, N1), (L1, L2), (L2, L1)))
    across = go(noted, ((N1, L1), (N2, L2), (L1, N1), (L2, N2)))
    crossed = go(noted, ((N1, L2), (N2, L1), (L1, N2), (L2, N1)))
    ghost = jax.ShapeDtypeStruct((3, T, T), BF16)
    near, far = pl.pallas_call(
        pick_kernel, out_shape=(ghost, ghost), in_specs=[SMEM, HBM], out_specs=(VMEM, VMEM),
        scratch_shapes=[pltpu.SemaphoreType.DMA((8,))], compiler_params=params(8), name="pick",
    )(send_rows, noted)
    near, far = swap_rows(near, 0, rows, cols), swap_rows(far, 1, rows, cols)
    turned = jax.ShapeDtypeStruct((BR, G * T, T), BF16)
    sums, rest = pl.pallas_call(
        product_kernel, out_shape=(turned, turned),
        in_specs=[SMEM, SMEM, FIXED, HBM, HBM, HBM], out_specs=(VMEM, VMEM),
        scratch_shapes=[pltpu.VMEM((BR, KA, T, T), BF16), pltpu.VMEM(((BR + 4) * G, T, T), BF16),
                        pltpu.VMEM((BR, T, T), BF16), pltpu.VMEM((2, 3, T, T), BF16),
                        pltpu.SemaphoreType.DMA((BR + 3,))],
        compiler_params=params(50), name="products",
    )(a_cols, ids, a_tiles, noted, near, far)
    travels = jax.ShapeDtypeStruct((2, G * T, T), BF16)
    near, far = pl.pallas_call(
        partial_kernel, out_shape=(travels, travels), in_specs=[VMEM] + [HBM] * 4, out_specs=(VMEM, VMEM),
        scratch_shapes=[pltpu.VMEM((2, BR + 1, T, T), BF16), pltpu.VMEM((2, BR * T, 2 * T), BF16),
                        pltpu.SemaphoreType.DMA((2,))],
        compiler_params=params(24), name="partials",
    )(sums, noted, swapped, across, crossed)
    near_sum, far_sum = swap_rows(near, 0, rows, cols), swap_rows(far, 1, rows, cols)
    out = jax.ShapeDtypeStruct((2, NCC, T, T), F32)
    zeroed, total = pl.pallas_call(
        local_kernel, out_shape=(out, jax.ShapeDtypeStruct((2, 4 * T, T), F32)),
        in_specs=[VMEM] * 2 + [HBM] * 5, out_specs=(HBM, VMEM),
        scratch_shapes=[pltpu.VMEM((2, BR + 1, T, T), BF16), pltpu.VMEM((8, T, T), F32),
                        pltpu.SemaphoreType.DMA((10,))],
        compiler_params=params(24), name="local",
    )(sums, rest, noted, swapped, across, crossed, near)
    return pl.pallas_call(
        final_kernel, out_shape=out, in_specs=[VMEM] * 3 + [HBM], out_specs=HBM,
        scratch_shapes=[pltpu.VMEM((2, 4, T, T), F32), pltpu.SemaphoreType.DMA((8,))],
        input_output_aliases={3: 0}, compiler_params=params(24), name="final",
    )(total, near_sum, far_sum, zeroed)


def solution(mesh):
    in_specs = (P("row", None, None, None), P("row", None), P("row", "col", None, None), P("row", "col"), P("row", None))
    body = functools.partial(shards, mesh.shape["row"], mesh.shape["col"])
    return jax.shard_map(body, mesh=mesh, in_specs=in_specs, out_specs=P("row", "col", None, None), check_vma=False)
```

```python
import functools

import jax
import jax.numpy as jnp
from jax import lax
from jax.experimental import pallas as pl
from jax.experimental.pallas import tpu as pltpu
from jax.sharding import PartitionSpec as P

T = 128
BR = 16
KA = 27
G = 3
UNROLL = 2
NCC = 32
F32 = jnp.float32
BF16 = jnp.bfloat16
MB = 1 << 20
SMEM = pl.BlockSpec(memory_space=pltpu.SMEM)
VMEM = pl.BlockSpec(memory_space=pltpu.VMEM)
HBM = pl.BlockSpec(memory_space=pl.ANY)
FIXED = pl.BlockSpec(memory_space=pltpu.HBM)


def place():
    s = lax.axis_index("row")
    c = lax.axis_index("col")
    d = lax.rem(c - 2 * s + 512, 4)
    is_n = d >= 2
    number = lax.rem(d, 2)
    return s, is_n, number, 2 * s - 4 + d


def roles(s):
    return (2, 3, 1, 0) if s % 2 == 0 else (0, 1, 3, 2)


def send(block, routes, rows, cols):
    pairs = []
    for s in range(rows):
        at = roles(s)
        pairs += [(s * cols + at[i], s * cols + at[j]) for i, j in routes]
    return lax.ppermute(block, ("row", "col"), pairs)


def swap_rows(block, odd, rows, cols):
    pairs = [(s, (s + 1) % rows if s % 2 == odd else (s - 1) % rows) for s in range(rows)]
    return lax.ppermute(block, "row", pairs)


N1, N2, L1, L2 = range(4)


def note_kernel(ids_ref, p_ref, all_ref, sem):
    copy = pltpu.make_async_copy(p_ref, all_ref.at[pl.ds(0, BR)], sem)
    copy.start()
    for i in range(BR):
        all_ref[BR, 8 * i:8 * i + 8, :] = jnp.full((8, T), ids_ref[i].astype(F32), F32).astype(BF16)
    copy.wait()


def pick_kernel(send_ref, p_ref, near_ref, far_ref, sems):
    odd = lax.rem(lax.axis_index("row"), 2)
    copies = []
    for d, out in ((odd, near_ref), (1 - odd, far_ref)):
        for t in range(2):
            row = send_ref[d, t]
            copies.append(pltpu.make_async_copy(p_ref.at[row], out.at[t], sems.at[len(copies)]))
            copies.append(pltpu.make_async_copy(p_ref.at[BR, pl.ds(pl.multiple_of(row * 8, 8), 8)],
                                                out.at[2, pl.ds(t * 8, 8)], sems.at[len(copies)]))
    for copy in copies:
        copy.start()
    for copy in copies:
        copy.wait()


def product_kernel(cols_ref, ids_ref, a_ref, own_ref, near_ref, far_ref, sums_ref, rest_ref, tiles, right, own, ghosts, sems):
    early = [pltpu.make_async_copy(own_ref.at[pl.ds(0, BR)], own, sems.at[BR]),
             pltpu.make_async_copy(near_ref, ghosts.at[0], sems.at[BR + 1]),
             pltpu.make_async_copy(far_ref, ghosts.at[1], sems.at[BR + 2])]
    for copy in early:
        copy.start()
    for i in range(BR):
        pltpu.make_async_copy(a_ref.at[i], tiles.at[i], sems.at[i]).start()
    s, is_n, number, first = place()
    right[...] = jnp.zeros_like(right)
    for copy in early:
        copy.wait()
    for j in range(BR):
        group = lax.rem(ids_ref[j] - first + 512, T) // 4
        right[j * G + group] = own[j]
    odd = lax.rem(s, 2)
    for side in range(2):
        base = BR + 2 * (1 - odd if side == 0 else odd)
        for t in range(2):
            ids = ghosts[side, 2, 8 * t:8 * t + 8, :].astype(F32)[:1]
            tile = ghosts[side, t].astype(F32)
            for g in range(G):
                wanted = lax.rem(first + 4 * g + T, T).astype(F32)
                right[(base + t) * G + g] = jnp.where(ids == wanted, tile, 0.0).astype(BF16)

    def one(i):
        pltpu.make_async_copy(a_ref.at[i], tiles.at[i], sems.at[i]).wait()
        rows = [cols_ref[i, m] * G for m in range(KA)]
        left = jnp.concatenate([tiles[i, m] for m in range(KA)], axis=1)
        both = jnp.concatenate(
            [jnp.concatenate([right[j + g] for g in range(G)], axis=1) for j in rows], axis=0)
        acc = jnp.dot(left, both, preferred_element_type=F32)
        turned = jnp.concatenate([acc[:, g * T:(g + 1) * T].T for g in range(G)], axis=0)
        high = turned.astype(BF16)
        sums_ref[i] = high
        rest_ref[i] = (turned - high.astype(F32)).astype(BF16)

    def step(n, _):
        for k in range(UNROLL):
            one(UNROLL * n + k)
        return 0

    lax.fori_loop(0, BR // UNROLL, step, 0)


def wide(ref):
    return jnp.concatenate([ref[i] for i in range(BR)], axis=1)


def partial_kernel(sums_ref, own, swapped, across, crossed, near_ref, far_ref, masked):
    s, is_n, number, first = place()
    odd = lax.rem(s, 2) == 1

    def add(tiles, row, n):
        wanted = lax.rem(2 * s - 2 + row + T, T).astype(F32)
        for i in range(BR):
            lower = jnp.where(tiles[BR, 8 * i:8 * i + 8, :].astype(F32)[:1] == wanted, 1.0, 0.0)
            masked[n, i * T:(i + 1) * T, :T] = tiles[i] * lower.astype(BF16)
            masked[n, i * T:(i + 1) * T, T:] = tiles[i] * (1.0 - lower).astype(BF16)
        terms = jnp.dot(wide(sums_ref), masked[n], preferred_element_type=F32)
        near_ref[row] = jnp.where(odd, terms[:, :T], terms[:, T:]).astype(BF16)
        far_ref[row] = jnp.where(odd, terms[:, T:], terms[:, :T]).astype(BF16)

    @pl.when(is_n)
    def _():
        add(own, number, 0)
        add(swapped, 1 - number, 1)

    @pl.when(jnp.logical_not(is_n))
    def _():
        add(across, 1 - number, 0)
        add(crossed, number, 1)


def local_kernel(sums_ref, rest_ref, own, swapped, across, crossed, after, out_ref, total_ref, zeros, sems):
    del after
    s, is_n, number, first = place()
    zeros[...] = jnp.zeros_like(zeros)
    copies = [pltpu.make_async_copy(zeros, out_ref.at[r, pl.ds(q, 8)], sems.at[r * 4 + q // 8])
              for r in range(2) for q in range(0, NCC, 8)]
    for copy in copies:
        copy.start()
    total_ref[...] = jnp.zeros_like(total_ref)
    at = pl.ds(pl.multiple_of(is_n.astype(jnp.int32) * T, T), G * T)

    def add(one, other, row):
        right = jnp.concatenate([x[:BR].reshape(BR * T, T) for x in (one, other)], axis=1)
        terms = jnp.dot(wide(sums_ref), right, preferred_element_type=F32)
        terms += jnp.dot(wide(rest_ref), right, preferred_element_type=F32)
        total_ref[row, at, :] = terms[:, :T]
        total_ref[1 - row, at, :] = terms[:, T:]

    @pl.when(is_n)
    def _():
        add(across, crossed, 1 - number)

    @pl.when(jnp.logical_not(is_n))
    def _():
        add(own, swapped, number)

    for copy in copies:
        copy.wait()


def final_kernel(total_ref, near_ref, far_ref, zeroed, out_ref, blocks, sems):
    del zeroed
    s, is_n, number, first = place()
    base = jnp.where(is_n, first - 4, first)
    odd = lax.rem(s, 2) == 1
    copies = []
    for r in range(2):
        for q in range(4):
            block = total_ref[r, q * T:(q + 1) * T, :]
            if q < G:
                at = slice(q * T, (q + 1) * T)
                block += jnp.where(odd, near_ref[r, at, :].astype(F32), far_ref[r, at, :].astype(F32))
            if q > 0:
                at = slice((q - 1) * T, q * T)
                block += jnp.where(odd, far_ref[r, at, :].astype(F32), near_ref[r, at, :].astype(F32))
            blocks[r, q] = block.T
            column = lax.rem(base + 4 * q + T, T) // 4
            copy = pltpu.make_async_copy(blocks.at[r, q], out_ref.at[r, column], sems.at[r * 4 + q])
            copy.start()
            copies.append(copy)
    for copy in copies:
        copy.wait()


def params(mib):
    return pltpu.CompilerParams(vmem_limit_bytes=mib * MB)


def cost(flops, count):
    return pl.CostEstimate(flops=flops, bytes_accessed=count, transcendentals=0)


def shards(rows, cols, a_tiles, a_cols, p_tiles, p_cols, send_rows):
    go = functools.partial(send, rows=rows, cols=cols)
    own = p_tiles.reshape(BR, T, T)
    ids = p_cols.reshape(BR)
    noted = pl.pallas_call(
        note_kernel, out_shape=jax.ShapeDtypeStruct((BR + 1, T, T), BF16), in_specs=[SMEM, FIXED], out_specs=VMEM,
        scratch_shapes=[pltpu.SemaphoreType.DMA], compiler_params=params(8), name="note",
    )(ids, own)
    swapped = go(noted, ((N1, N2), (N2, N1), (L1, L2), (L2, L1)))
    across = go(noted, ((N1, L1), (N2, L2), (L1, N1), (L2, N2)))
    crossed = go(noted, ((N1, L2), (N2, L1), (L1, N2), (L2, N1)))
    ghost = jax.ShapeDtypeStruct((3, T, T), BF16)
    near, far = pl.pallas_call(
        pick_kernel, out_shape=(ghost, ghost), in_specs=[SMEM, HBM], out_specs=(VMEM, VMEM),
        scratch_shapes=[pltpu.SemaphoreType.DMA((8,))], compiler_params=params(8), name="pick",
    )(send_rows, noted)
    near, far = swap_rows(near, 0, rows, cols), swap_rows(far, 1, rows, cols)
    turned = jax.ShapeDtypeStruct((BR, G * T, T), BF16)
    sums, rest = pl.pallas_call(
        product_kernel, out_shape=(turned, turned),
        in_specs=[SMEM, SMEM, FIXED, HBM, HBM, HBM], out_specs=(VMEM, VMEM),
        scratch_shapes=[pltpu.VMEM((BR, KA, T, T), BF16), pltpu.VMEM(((BR + 4) * G, T, T), BF16),
                        pltpu.VMEM((BR, T, T), BF16), pltpu.VMEM((2, 3, T, T), BF16),
                        pltpu.SemaphoreType.DMA((BR + 3,))],
        compiler_params=params(50), name="products",
    )(a_cols, ids, a_tiles, noted, near, far)
    travels = jax.ShapeDtypeStruct((2, G * T, T), BF16)
    near, far = pl.pallas_call(
        partial_kernel, out_shape=(travels, travels), in_specs=[VMEM] * 5, out_specs=(VMEM, VMEM),
        scratch_shapes=[pltpu.VMEM((2, BR * T, 2 * T), BF16)],
        compiler_params=params(24), name="partials",
    )(sums, noted, swapped, across, crossed)
    near_sum, far_sum = swap_rows(near, 0, rows, cols), swap_rows(far, 1, rows, cols)
    out = jax.ShapeDtypeStruct((2, NCC, T, T), F32)
    zeroed, total = pl.pallas_call(
        local_kernel, out_shape=(out, jax.ShapeDtypeStruct((2, 4 * T, T), F32)),
        in_specs=[VMEM] * 6 + [HBM], out_specs=(HBM, VMEM),
        scratch_shapes=[pltpu.VMEM((8, T, T), F32), pltpu.SemaphoreType.DMA((8,))],
        compiler_params=params(24), name="local",
    )(sums, rest, noted, swapped, across, crossed, near)
    return pl.pallas_call(
        final_kernel, out_shape=out, in_specs=[VMEM] * 3 + [HBM], out_specs=HBM,
        scratch_shapes=[pltpu.VMEM((2, 4, T, T), F32), pltpu.SemaphoreType.DMA((8,))],
        input_output_aliases={3: 0}, compiler_params=params(24), name="final",
    )(total, near_sum, far_sum, zeroed)


def solution(mesh):
    in_specs = (P("row", None, None, None), P("row", None), P("row", "col", None, None), P("row", "col"), P("row", None))
    body = functools.partial(shards, mesh.shape["row"], mesh.shape["col"])
    return jax.shard_map(body, mesh=mesh, in_specs=in_specs, out_specs=P("row", "col", None, None), check_vma=False)
```
